32 devices in a mesh: seq: 32 (over z, y, x, core), head: 1.
Axes of the slice: x: 2, y: 2, z: 4, core: 2. Of those that a mesh axis runs over, the one named last changes fastest.
Arguments:
- x_in: bfloat16 [16384, 4096], P('seq', 'head'), may hold values from -6 to 6
- gate_input: bfloat16 [16384, 4096], P('seq', 'head'), may hold values from -6 to 6
- in_b: bfloat16 [16384, 512], P('seq', 'head'), may hold values from -2 to 2
- in_c: bfloat16 [16384, 512], P('seq', 'head'), may hold values from -2 to 2
- step_size: float32 [16384, 64], P('seq', 'head'), may hold values from 0.02 to 0.2
- log_decay: float32 [16384, 64], P('seq', 'head'), may hold values from -0.7 to 0, as said below
- skip_gain: float32 [64], P('head'), may hold values from 0.5 to 1.5
- norm_gain: float32 [4096], P('head'), may hold values from 0.5 to 1.5
- out_weight: bfloat16 [4096, 8192], P('head', 'seq'), may hold values from -0.046875 to 0.046875
- probe: bfloat16 [32, 8192, 128], P('seq', 'head'), may hold values from -0.29882812 to 0.29882812
- span_start: int32 [2048], P('seq'), may hold values from 0 to 16383, as said below
- span_len: int32 [2048], P('seq'), may hold values from 1 to 128, as said below
- span_owner: int32 [2048, 1], P('seq'), may hold values from 0 to 31; in each aligned block of 64 rows (0 to 63, 64 to 127, ...) at most 2 rows name the same one
- span_label: int32 [2048], P('seq'), may hold values from 0 to 127
Outputs:
- layer_out: bfloat16 [16384, 8192], P('seq', 'head')
- probe_grad: float32 [32, 8192, 128], P('seq', 'head')
- slot_loss: float32 [32, 64], P('seq')
The draws below stay inside these ranges and needn't reach their ends.
Inputs may be any that keep to these rules, and one draw needn't show every extreme that they name: `log_decay`: log of a decay factor in (0, 1]. Span i starts among tokens (i // 64) * 512 to (i // 64 + 1) * 512 - 1, and span_start + span_len <= 16384. `span_len`: the first span of every block of 64 spans is 128 long. `span_owner`: in each aligned block of 64 spans no owner appears more than 2 times.
All inputs are finite; a program needn't handle non-finite values.
Results may differ from the reference program's by a relative error of at most 0.0068.
Values may be sent and summed in bfloat16 or wider, within the bound.
A program may use at most 256 MiB of HBM per device.

```python
import math
import jax
import jax.numpy as jnp
import numpy as np
from jax import lax

D = 8192
HEADS = 64
HEAD_DIM = 64
STATE = 128
GROUPS = 4
LABELS = 128
TOK_DEV = 512
SPAN_DEV = 64
CAP = 2
SPAN_MAX = 128
INNER = 4096
TOKENS = 16384
SPANS = 2048
SLOTS = 64
N_SEQ = 32
N_HEAD = 1


def draw_log_decay(key, part):
    keys = jax.random.split(key, 6)
    slow = jax.random.randint(keys[0], (HEADS,), 0, 10) < 5
    rate_slow = jnp.exp(jax.random.uniform(keys[1], (HEADS,), jnp.float32, math.log(0.1 / TOKENS), math.log(0.5 / TOKENS)))
    rate_fast = jnp.exp(jax.random.uniform(keys[2], (HEADS,), jnp.float32, math.log(1.0 / 50.0), math.log(1.0 / 15.0)))
    forgetting_speed = jnp.where(slow, rate_slow, rate_fast)
    approximate_guess = jax.random.uniform(keys[3], (TOKENS, HEADS), jnp.float32, 0.5, 1.5)
    places = jax.random.randint(keys[4], (3,), 0, TOKENS)
    stacking_level = jax.random.uniform(keys[5], (3, HEADS), jnp.float32, 0.22, 0.5)
    interval_covered_flags = (jnp.arange(TOKENS)[:, None] == places[None, :]).astype(jnp.float32)
    spike_magnitude = jnp.dot(interval_covered_flags, stacking_level)
    return -(forgetting_speed[None, :] * approximate_guess + spike_magnitude)


def span_pair(key):
    inner = jax.random.fold_in(key, 7)
    keys = jax.random.split(inner, 2)
    offsets = jax.random.randint(keys[0], (N_SEQ, SPAN_DEV), 0, TOK_DEV)
    lengths = jax.random.randint(keys[1], (N_SEQ, SPAN_DEV), 1, SPAN_MAX + 1)
    lengths = lengths.at[:, 0].set(SPAN_MAX)
    starts = jnp.arange(N_SEQ, dtype=jnp.int32)[:, None] * TOK_DEV + offsets
    starts = jnp.minimum(starts, TOKENS - lengths)
    return (starts.reshape(-1).astype(jnp.int32), lengths.reshape(-1).astype(jnp.int32))


def draw_span_start(key, part):
    return span_pair(key)[0]


def draw_span_len(key, part):
    return span_pair(key)[1]


def plant(array, rng, smallest, largest):
    index_at = [jax.random.randint(jax.random.fold_in(rng, axis), (), 0, length) for axis, length in enumerate(array.shape)]
    main_axis = array.shape.index(max(array.shape))
    neighbour = index_at[:main_axis] + [(index_at[main_axis] + 1) % array.shape[main_axis]] + index_at[main_axis + 1:]
    return array.at[tuple(index_at)].set(smallest).at[tuple(neighbour)].set(largest)


def block_scale(rng, extent, pieces, low, high):
    def one(position, parts):
        draws = jax.random.uniform(jax.random.fold_in(jax.random.fold_in(rng, 6), position), (parts,), jnp.float32, low / len(pieces), high / len(pieces))
        return jnp.repeat(jnp.exp(draws), extent[position] // parts).reshape((-1,) + (1,) * (len(extent) - position - 1))

    loudness = one(*pieces[0])
    for cut in pieces[1:]:
        loudness = loudness * one(*cut)
    return loudness


def shared_out(rng, own, number, rows, count, top, limit, slope):
    ranking = jax.random.permutation(rng, count)
    heavy_load, usual = shares(count, rows * top, limit, slope, True), shares(count, rows * top, limit, slope, False)
    places = jnp.arange(count)

    def named(tallies, turn):
        used = int((tallies > 0).sum())
        fixed = max(1, used // 4)
        moved = fixed + (places - fixed + turn * (used - fixed)) % max(1, count - fixed)
        return jnp.zeros((count,), jnp.int32).at[ranking[jnp.where(places < fixed, places, moved)]].set(jnp.asarray(tallies, jnp.int32))

    tallies = jnp.where(number % 4 == 0, named(heavy_load, number // 4), named(usual, number - number // 4 - 1))
    mixed = jax.random.permutation(jax.random.fold_in(own, 3), count)
    source_of, taker = mixed[0:count // 2 * 2:2], mixed[1:count // 2 * 2:2]
    slack = jnp.minimum(tallies[source_of] - 1, limit - tallies[taker]) // 2
    slack = jnp.where((source_of == ranking[0]) | (taker == ranking[0]) | (tallies[taker] == 0), 0, jnp.maximum(slack, 0))
    moved = jax.random.randint(jax.random.fold_in(own, 4), (count // 2,), 0, 1 << 20) % (slack + 1)
    tallies = tallies.at[source_of].add(-moved).at[taker].add(moved)
    items = jnp.searchsorted(jnp.cumsum(tallies), jnp.arange(rows * top), side="right").astype(jnp.int32)
    listing = items.reshape(top, rows).T
    listing = listing[jax.random.permutation(jax.random.fold_in(own, 1), rows)]
    turn = jax.random.randint(jax.random.fold_in(own, 2), (rows, 1), 0, top)
    return jnp.take_along_axis(listing, (jnp.arange(top)[None, :] + turn) % top, axis=1)


def shares(amount, total, reach, lean, full):
    weights = [(1 << 20) // math.isqrt(grade ** lean) + 1 for grade in range(1, amount + 1)]
    largest = reach if full else min(reach, max(-(-total // amount), total * weights[0] // sum(weights)))
    least = 1 if total - largest >= amount - 1 else 0
    given, rest = [largest] + [least] * (amount - 1), total - largest - least * (amount - 1)
    while rest > 0:
        candidates = [i for i in range(1, amount) if given[i] < largest] or [i for i in range(1, amount) if given[i] < reach]
        whole, remaining = sum([weights[i] for i in candidates]), rest
        for i in candidates:
            more = min(reach - given[i], max(1, remaining * weights[i] // whole), rest)
            given[i] = given[i] + more
            rest = rest - more
    return np.array(given)


def noise(stream_key, dims, width, bound, cuts=(), kind=jnp.bfloat16):
    gain = block_scale(stream_key, dims, cuts, -0.22, 0.18) if cuts else 1.0
    values = jax.random.normal(stream_key, dims, jnp.float32) * width * gain
    return jnp.minimum(jnp.maximum(values, -bound), bound).astype(kind)


def setup_inputs(seed: int = 0) -> dict:
    streams_of = jax.random.split(jax.random.key(seed), 15)
    x_in = noise(streams_of[0], (TOKENS, INNER), 1.0, 6.0, ((0, 32),))
    gate_input = noise(streams_of[1], (TOKENS, INNER), 1.0, 6.0, ((0, 32),))
    in_b = noise(streams_of[2], (TOKENS, GROUPS * STATE), 0.3, 2.0, ((0, 32),))
    in_c = noise(streams_of[3], (TOKENS, GROUPS * STATE), 0.3, 2.0, ((0, 32),))
    step_size = jnp.clip(jnp.exp(math.log(0.2) - 2.3025851 * jax.random.uniform(streams_of[4], (TOKENS, HEADS), jnp.float32) ** block_scale(streams_of[4], (TOKENS, HEADS), ((0, 32),), -0.2, 0.2)), 0.02, 0.2)
    log_decay = draw_log_decay(jax.random.fold_in(streams_of[14], 71), 0)
    skip_gain = jnp.clip(jax.random.uniform(streams_of[6], (HEADS,), jnp.float32, 0.5, 1.5), 0.5, 1.5)
    norm_gain = jnp.clip(1.0 + 0.1 * jax.random.normal(streams_of[7], (INNER,), jnp.float32), 0.5, 1.5)
    out_weight = noise(streams_of[8], (INNER, D), (4 * INNER) ** -0.5, 0.046875, ((1, 32),))
    probe = noise(streams_of[9], (N_SEQ, D, LABELS), 0.05, 0.29882812, ((0, 32),))
    span_start = draw_span_start(jax.random.fold_in(streams_of[14], 71), 0)
    span_len = draw_span_len(jax.random.fold_in(streams_of[14], 71), 0)
    span_owner_keys = jax.random.split(jax.random.fold_in(streams_of[12], 1), SPANS // SPAN_DEV)
    span_owner_turns = jax.random.permutation(jax.random.fold_in(streams_of[12], 3), SPANS // SPAN_DEV)
    span_owner = jax.vmap(lambda own, number: shared_out(jax.random.fold_in(streams_of[12], 2), own, number, SPAN_DEV, N_SEQ, 1, CAP, 2))(span_owner_keys, span_owner_turns).reshape((SPANS, 1))
    span_label = plant(jax.random.randint(streams_of[13], (SPANS,), 0, LABELS), jax.random.fold_in(streams_of[13], 1), 0, LABELS - 1).astype(jnp.int32)
    return {"x_in": x_in, "gate_input": gate_input, "in_b": in_b, "in_c": in_c, "step_size": step_size, "log_decay": log_decay, "skip_gain": skip_gain, "norm_gain": norm_gain, "out_weight": out_weight, "probe": probe, "span_start": span_start, "span_len": span_len, "span_owner": span_owner, "span_label": span_label}


def segment_summands(xs, bmat, cmat, dtk, cum):
    high = lax.Precision.HIGHEST
    tok = xs.shape[0]
    cb = jnp.einsum('tgn,sgn->gts', cmat, bmat, precision=high)
    ordered = jnp.transpose(cum, (1, 2, 0))
    diff = ordered[:, :, :, None] - ordered[:, :, None, :]
    lower = jnp.arange(tok)[:, None] >= jnp.arange(tok)[None, :]
    decay = jnp.where(lower, jnp.exp(jnp.where(lower, diff, 0.0)), 0.0)
    weights = cb[:, None] * decay * jnp.transpose(dtk, (1, 2, 0))[:, :, None, :]
    intra = jnp.einsum('gkts,sgkp->tgkp', weights, xs, precision=high)
    tail = jnp.exp(cum[-1][None] - cum) * dtk
    local_state = jnp.einsum('tgk,tgkp,tgn->gkpn', tail, xs, bmat, precision=high)
    return (intra, local_state, cum[-1])

def inter_term(cmat, cum, state_in):
    high = lax.Precision.HIGHEST
    return jnp.exp(cum)[..., None] * jnp.einsum('tgn,gkpn->tgkp', cmat, state_in, precision=high)

def reference(x_in, gate_input, in_b, in_c, step_size, log_decay, skip_gain, norm_gain, out_weight, probe, span_start, span_len, span_owner, span_label):
    per_group = HEADS // GROUPS
    xs = x_in.astype(jnp.float32).reshape(N_SEQ, TOK_DEV, GROUPS, per_group, HEAD_DIM)
    bmat = in_b.astype(jnp.float32).reshape(N_SEQ, TOK_DEV, GROUPS, STATE)
    cmat = in_c.astype(jnp.float32).reshape(N_SEQ, TOK_DEV, GROUPS, STATE)
    dtk = step_size.reshape(N_SEQ, TOK_DEV, GROUPS, per_group)
    cum = jnp.cumsum(log_decay.reshape(N_SEQ, TOK_DEV, GROUPS, per_group), axis=1)

    def advance(state, block):
        xb, bb, cb, db, qb = block
        intra, local_state, total = segment_summands(xb, bb, cb, db, qb)
        result = intra + inter_term(cb, qb, state)
        fresh = state * jnp.exp(total)[..., None, None] + local_state
        return (fresh, result)
    start_state = jnp.zeros((GROUPS, per_group, HEAD_DIM, STATE), jnp.float32)
    unused, ssm = lax.scan(advance, start_state, (xs, bmat, cmat, dtk, cum))
    ssm = ssm + skip_gain.reshape(GROUPS, per_group)[None, None, :, :, None] * xs
    ssm = ssm.reshape(TOKENS, GROUPS, per_group * HEAD_DIM)
    gated = ssm * jax.nn.silu(gate_input.astype(jnp.float32).reshape(TOKENS, GROUPS, per_group * HEAD_DIM))
    meansq = lax.optimization_barrier(jnp.mean(gated * gated, axis=-1, keepdims=True))
    normalized_input = gated * lax.rsqrt(meansq + 1e-05)
    y_out = (normalized_input.reshape(TOKENS, INNER) * norm_gain[None, :]).astype(jnp.bfloat16)
    rows_half = INNER // N_HEAD
    total = jnp.zeros((TOKENS, D), jnp.float32)
    for half in range(N_HEAD):
        part = jnp.dot(y_out[:, half * rows_half:(half + 1) * rows_half], out_weight[half * rows_half:(half + 1) * rows_half], preferred_element_type=jnp.float32)
        part = lax.optimization_barrier(part.astype(jnp.bfloat16)).astype(jnp.float32)
        total = total + part
    layer_out = total.astype(jnp.bfloat16)
    padded = jnp.concatenate([layer_out, jnp.zeros((SPAN_MAX, D), jnp.bfloat16)], axis=0)

    def pool(pair):
        first, length = pair
        rows = lax.dynamic_slice_in_dim(padded, first.astype(jnp.int32), SPAN_MAX, 0).astype(jnp.float32)
        keep = jnp.arange(SPAN_MAX) < length
        return lax.optimization_barrier(jnp.sum(jnp.where(keep[:, None], rows, 0.0), axis=0))
    sums = lax.map(pool, (span_start, span_len))
    feature = (sums / span_len[:, None].astype(jnp.float32)).astype(jnp.bfloat16)
    owners = span_owner[:, 0].reshape(N_SEQ, SPAN_DEV)
    index = jnp.arange(SPAN_DEV)
    earlier = index[None, :] < index[:, None]
    same = owners[:, :, None] == owners[:, None, :]
    slot = lax.optimization_barrier(jnp.sum(jnp.logical_and(same, earlier[None]), axis=-1)).astype(jnp.int32)
    matrix_column_index = (jnp.arange(N_SEQ, dtype=jnp.int32)[:, None] * CAP + slot).reshape(-1).astype(jnp.int32)
    table = jnp.full((N_SEQ, SLOTS), -1, jnp.int32).at[span_owner[:, 0], matrix_column_index].set(jnp.arange(SPANS, dtype=jnp.int32))

    def score(owner):
        ids = table[owner]
        valid = ids >= 0
        safe = jnp.maximum(ids, 0)
        feats = jnp.where(valid[:, None], feature[safe], jnp.zeros((), jnp.bfloat16))
        labels = jnp.where(valid, span_label[safe], -1)
        logits = jnp.dot(feats, probe[owner], preferred_element_type=jnp.float32)
        top = lax.optimization_barrier(jnp.max(logits, axis=1, keepdims=True))
        lse = top[:, 0] + jnp.log(lax.optimization_barrier(jnp.sum(jnp.exp(logits - top), axis=1)))
        onehot = jnp.arange(LABELS)[None, :] == labels[:, None]
        picked = lax.optimization_barrier(jnp.sum(jnp.where(onehot, logits, 0.0), axis=1))
        loss = jnp.where(valid, lse - picked, 0.0)
        probs = jnp.exp(logits - lse[:, None])
        resid = jnp.where(valid[:, None], probs - onehot.astype(jnp.float32), 0.0).astype(jnp.bfloat16)
        grad = jnp.dot(feats.T, resid, preferred_element_type=jnp.float32)
        return (grad, loss)
    probe_grad, slot_loss = lax.map(score, jnp.arange(N_SEQ, dtype=jnp.int32))
    return (layer_out, probe_grad, slot_loss)
```

```python
import functools

import jax
import jax.numpy as jnp
from jax import lax
from jax.experimental import pallas as pl
from jax.experimental.pallas import tpu as pltpu
from jax.sharding import PartitionSpec as P

HEAD_DIM = 64
STATE = 128
CAP = 2
CHUNK = 128
PAIR = 2 * HEAD_DIM
META = 16
F32 = jnp.float32
BF16 = jnp.bfloat16


def from_behind(value, axis, steps):
    count = lax.axis_size(axis)
    leading, last = (max(0, -steps), min(count, count - steps))
    return lax.ppermute(value, axis, [(source, source + steps) for source in range(leading, last)])


def inside_mask(first, length, place):
    return jnp.logical_and(
        place[None, :] >= first[:, None], place[None, :] < (first + length)[:, None]
    ).astype(BF16)


def pair_of(cols, p, rows):
    low = lax.broadcasted_iota(jnp.int32, (rows, PAIR), 1) < HEAD_DIM
    a = jnp.broadcast_to(cols[:, 2 * p : 2 * p + 1], (rows, PAIR))
    b = jnp.broadcast_to(cols[:, 2 * p + 1 : 2 * p + 2], (rows, PAIR))
    return jnp.where(low, a, b)


def local_kernel(pairs, x_ref, b_ref, tail_ref, meta_ref, out_ref):
    rows = x_ref.shape[0]
    tail = tail_ref[0]
    scaled = [
        (x_ref[:, PAIR * p : PAIR * (p + 1)].astype(F32) * pair_of(tail, p, rows)).astype(BF16)
        for p in range(pairs)
    ]
    state = lax.dot_general(
        b_ref[...],
        jnp.concatenate(scaled, axis=1),
        (((0,), (0,)), ((), ())),
        preferred_element_type=F32,
    )
    for p in range(pairs):
        out_ref[p, :STATE, :] = state[:, PAIR * p : PAIR * (p + 1)].astype(BF16)
        out_ref[p, STATE:, :] = meta_ref[p]


def local_states(x_in, in_b, tail, meta, groups, pairs):
    tok = x_in.shape[0]
    width = pairs * PAIR
    return pl.pallas_call(
        functools.partial(local_kernel, pairs),
        grid=(groups,),
        in_specs=[
            pl.BlockSpec((tok, width), lambda g: (0, g)),
            pl.BlockSpec((tok, STATE), lambda g: (0, g)),
            pl.BlockSpec((1, tok, 2 * pairs), lambda g: (g, 0, 0)),
            pl.BlockSpec((pairs, META, PAIR), lambda g: (g, 0, 0)),
        ],
        out_specs=pl.BlockSpec((pairs, STATE + META, PAIR), lambda g: (g, 0, 0)),
        out_shape=jax.ShapeDtypeStruct((groups * pairs, STATE + META, PAIR), BF16),
        name="local_states",
        compiler_params=pltpu.CompilerParams(vmem_limit_bytes=40 * 2**20),
    )(x_in, in_b, tail, meta)


def prefix_kernel(per, got_ref, out_ref):
    count = got_ref.shape[0] // per
    for q in range(per):
        state = jnp.zeros((STATE, PAIR), F32)
        for k in range(count):
            out_ref[k * per + q] = state.astype(BF16)
            block = got_ref[k * per + q].astype(F32)
            keep = jnp.exp(block[STATE : STATE + 1] + block[STATE + 1 : STATE + 2])
            state = state * keep + block[:STATE]


def prefix_states(got, per):
    return pl.pallas_call(
        functools.partial(prefix_kernel, per),
        out_shape=jax.ShapeDtypeStruct((got.shape[0], STATE, PAIR), BF16),
        name="prefix_states",
        compiler_params=pltpu.CompilerParams(vmem_limit_bytes=40 * 2**20),
    )(got)


def mixer_kernel(
    pairs,
    x_ref,
    gate_ref,
    b_ref,
    c_ref,
    cum_ref,
    cumt_ref,
    dt_ref,
    skip_ref,
    gain_ref,
    in_ref,
    y_ref,
    state,
    gated,
):
    rows = x_ref.shape[0]

    @pl.when(pl.program_id(1) == 0)
    def _():
        state[...] = in_ref[...].astype(F32)

    bmat, cmat = b_ref[...], c_ref[...]
    cb = lax.dot_general(cmat, bmat, (((1,), (1,)), ((), ())), preferred_element_type=F32)
    row = lax.broadcasted_iota(jnp.int32, (rows, rows), 0)
    col = lax.broadcasted_iota(jnp.int32, (rows, rows), 1)
    cb = jnp.where(row >= col, cb, 0.0)
    low = lax.broadcasted_iota(jnp.int32, (rows, PAIR), 1) < HEAD_DIM
    cum, dt, cumt = cum_ref[0], dt_ref[0], cumt_ref[...]
    square = jnp.zeros((rows, 1), F32)
    for p in range(pairs):
        lanes = slice(PAIR * p, PAIR * (p + 1))
        x = x_ref[:, lanes].astype(F32)
        left = jnp.broadcast_to(cum[:, 2 * p : 2 * p + 1], (rows, PAIR))
        right = jnp.broadcast_to(cum[:, 2 * p + 1 : 2 * p + 2], (rows, PAIR))
        w0 = cb * jnp.exp(jnp.minimum(left - cumt[2 * p : 2 * p + 1, :], 0.0))
        w1 = cb * jnp.exp(jnp.minimum(right - cumt[2 * p + 1 : 2 * p + 2, :], 0.0))
        both = jnp.where(low, left, right)
        last = both[rows - 1 : rows, :]
        stepped = x * pair_of(dt, p, rows)
        stacked = jnp.concatenate(
            [jnp.where(low, stepped, 0.0), jnp.where(low, 0.0, stepped)], axis=0
        ).astype(BF16)
        weights = jnp.concatenate([w0, w1], axis=1).astype(BF16)
        held = state[p]
        result = jnp.dot(weights, stacked, preferred_element_type=F32)
        result += jnp.exp(both) * jnp.dot(cmat, held.astype(BF16), preferred_element_type=F32)
        result += skip_ref[0:1, lanes] * x
        ending = (stepped * jnp.exp(last - both)).astype(BF16)
        state[p] = held * jnp.exp(last) + lax.dot_general(
            bmat, ending, (((0,), (0,)), ((), ())), preferred_element_type=F32
        )
        g = gate_ref[:, lanes].astype(F32)
        u = result * (g / (1.0 + jnp.exp(-g)))
        gated[:, lanes] = u
        square += jnp.sum(u * u, axis=1, keepdims=True)
    scale = lax.rsqrt(square * (1.0 / (pairs * PAIR)) + 1e-05)
    y_ref[...] = (gated[...] * scale * gain_ref[0:1, :]).astype(BF16)


def mixer(x_in, gate, in_b, in_c, cum, cumt, dt, skip, gain, incoming, groups, pairs):
    tok = x_in.shape[0]
    width = pairs * PAIR
    wide = pl.BlockSpec((CHUNK, width), lambda g, c: (c, g))
    maps = pl.BlockSpec((CHUNK, STATE), lambda g, c: (c, g))
    cols = pl.BlockSpec((1, CHUNK, 2 * pairs), lambda g, c: (g, c, 0))
    line = pl.BlockSpec((1, width), lambda g, c: (0, g))
    return pl.pallas_call(
        functools.partial(mixer_kernel, pairs),
        grid=(groups, tok // CHUNK),
        in_specs=[
            wide,
            wide,
            maps,
            maps,
            cols,
            pl.BlockSpec((2 * pairs, CHUNK), lambda g, c: (g, c)),
            cols,
            line,
            line,
            pl.BlockSpec((pairs, STATE, PAIR), lambda g, c: (g, 0, 0)),
        ],
        out_specs=wide,
        out_shape=jax.ShapeDtypeStruct((tok, groups * width), BF16),
        scratch_shapes=[pltpu.VMEM((pairs, STATE, PAIR), F32), pltpu.VMEM((CHUNK, width), F32)],
        name="mixer",
        compiler_params=pltpu.CompilerParams(vmem_limit_bytes=40 * 2**20),
    )(x_in, gate, in_b, in_c, cum, cumt, dt, skip, gain, incoming)


def on_device(
    x_in,
    gate_input,
    in_b,
    in_c,
    step_size,
    log_decay,
    skip_gain,
    norm_gain,
    out_weight,
    probe,
    span_start,
    span_len,
    span_owner,
    span_label,
):
    tok, inner = x_in.shape
    heads = step_size.shape[1]
    groups = in_b.shape[1] // STATE
    pairs = heads // groups // 2
    owners = lax.axis_size("seq")
    weight = lax.all_gather(out_weight, "seq", axis=1, tiled=True)

    high = lax.Precision.HIGHEST
    lower = jnp.tril(jnp.ones((CHUNK, CHUNK), F32))
    cum = jnp.einsum("ts,csh->cth", lower, log_decay.reshape(-1, CHUNK, heads), precision=high)
    ends = cum[:, -1, :]
    total = jnp.sum(ends, axis=0)
    chunks = tok // CHUNK
    behind = jnp.stack(
        [sum((ends[j] for j in range(c + 1, chunks)), jnp.zeros_like(total)) for c in range(chunks)]
    )
    tail = jnp.exp(ends[:, None] - cum + behind[:, None]).reshape(tok, heads) * step_size
    cum = cum.reshape(tok, heads)

    def by_group(a):
        return jnp.transpose(a.reshape(tok, groups, 2 * pairs), (1, 0, 2))

    total_high = lax.reduce_precision(total, 8, 7)
    total_low = total - total_high
    halves = jnp.stack([total_high, total_low])
    wide = jnp.repeat(halves.reshape(2, heads // 2, 2), HEAD_DIM, axis=2)
    meta = jnp.pad(jnp.transpose(wide, (1, 0, 2)), ((0, 0), (0, META - 2), (0, 0))).astype(BF16)
    local = local_states(x_in, in_b, by_group(tail), meta, groups, pairs)

    here = heads // 2
    share = -(-here // owners)
    if share * owners > here:
        local = jnp.pad(local, ((0, share * owners - here), (0, 0), (0, 0)))
    got = lax.all_to_all(local, "seq", split_axis=0, concat_axis=0, tiled=True)
    incoming = lax.all_to_all(
        prefix_states(got, share), "seq", split_axis=0, concat_axis=0, tiled=True
    )[:here]
    skip = jnp.repeat(skip_gain, HEAD_DIM)[None]
    y = mixer(
        x_in,
        gate_input,
        in_b,
        in_c,
        by_group(cum),
        cum.T,
        by_group(step_size),
        skip,
        norm_gain[None],
        incoming,
        groups,
        pairs,
    )

    base = lax.axis_index("seq") * tok
    prev_start, prev_len = from_behind((span_start, span_len), "seq", 1)
    place = base + jnp.arange(tok, dtype=jnp.int32)
    count = span_start.shape[0]
    masks = jnp.concatenate(
        [inside_mask(prev_start, prev_len, place), inside_mask(span_start, span_len, place)]
    )
    both = jnp.dot(masks, y, preferred_element_type=F32)
    returned = from_behind(both[:count].astype(BF16), "seq", -1)
    means = (both[count:] + returned.astype(F32)) / span_len[:, None].astype(F32)
    slots_total = owners * CAP
    owner = span_owner[:, 0]
    index = jnp.arange(count)
    earlier = index[None, :] < index[:, None]
    same = owner[:, None] == owner[None, :]
    slot = jnp.sum(jnp.logical_and(same, earlier), axis=1)
    pick = jnp.arange(slots_total, dtype=jnp.int32)[:, None] == (owner * CAP + slot)[None, :]
    sent = jnp.dot(pick.astype(BF16), means.astype(BF16), preferred_element_type=F32)
    labels = jnp.sum(jnp.where(pick, span_label[None, :] + 1, 0), axis=1) - 1
    got_means = lax.all_to_all(
        sent.astype(BF16).reshape(owners, CAP, -1), "seq", split_axis=0, concat_axis=0, tiled=True
    ).reshape(slots_total, -1)
    labels = lax.all_to_all(
        labels.reshape(owners, CAP), "seq", split_axis=0, concat_axis=0, tiled=True
    ).reshape(-1)
    valid = labels >= 0

    return project(jnp.concatenate([y, got_means], axis=0), weight, probe, tok, labels, valid)


def project(rows, weight, probe, tok, labels, valid):
    out = jnp.dot(rows, weight, preferred_element_type=F32)
    if lax.axis_size("head") > 1:
        layer_out = lax.psum_scatter(
            out[:tok].astype(BF16), "head", scatter_dimension=1, tiled=True
        )
        feature = lax.psum_scatter(out[tok:], "head", scatter_dimension=1, tiled=True)
        feature = feature.astype(BF16)
    else:
        out = out.astype(BF16)
        layer_out, feature = out[:tok], out[tok:]
    logits = jnp.dot(feature, probe[0], preferred_element_type=F32)
    logits = lax.psum(logits, "head")
    top = jnp.max(logits, axis=1, keepdims=True)
    lse = top[:, 0] + jnp.log(jnp.sum(jnp.exp(logits - top), axis=1))
    onehot = jnp.arange(logits.shape[1])[None, :] == labels[:, None]
    picked = jnp.sum(jnp.where(onehot, logits, 0.0), axis=1)
    loss = jnp.where(valid, lse - picked, 0.0)
    probs = jnp.exp(logits - lse[:, None])
    resid = jnp.where(valid[:, None], probs - onehot.astype(F32), 0.0).astype(BF16)
    grad = jnp.dot(feature.T, resid, preferred_element_type=F32)
    return (layer_out, grad[None], loss[None])


def solution(mesh):
    placed = (
        P("seq", "head"),
        P("seq", "head"),
        P("seq", "head"),
        P("seq", "head"),
        P("seq", "head"),
        P("seq", "head"),
        P("head"),
        P("head"),
        P("head", "seq"),
        P("seq", "head", None),
        P("seq"),
        P("seq"),
        P("seq", None),
        P("seq"),
    )
    return jax.shard_map(
        on_device,
        mesh=mesh,
        in_specs=placed,
        out_specs=(P("seq", "head"), P("seq", "head", None), P("seq", None)),
        check_vma=False,
    )
```

```python
import functools

import jax
import jax.numpy as jnp
from jax import lax
from jax.experimental import pallas as pl
from jax.experimental.pallas import tpu as pltpu
from jax.sharding import PartitionSpec as P

HEAD_DIM = 64
STATE = 128
CAP = 2
CHUNK = 128
PAIR = 2 * HEAD_DIM
META = 16
F32 = jnp.float32
BF16 = jnp.bfloat16


def from_behind(value, axis, steps):
    count = lax.axis_size(axis)
    leading, last = (max(0, -steps), min(count, count - steps))
    return lax.ppermute(value, axis, [(source, source + steps) for source in range(leading, last)])


def inside_mask(first, length, place):
    return jnp.logical_and(
        place[None, :] >= first[:, None], place[None, :] < (first + length)[:, None]
    ).astype(BF16)


def pair_of(cols, p, rows):
    low = lax.broadcasted_iota(jnp.int32, (rows, PAIR), 1) < HEAD_DIM
    a = jnp.broadcast_to(cols[:, 2 * p : 2 * p + 1], (rows, PAIR))
    b = jnp.broadcast_to(cols[:, 2 * p + 1 : 2 * p + 2], (rows, PAIR))
    return jnp.where(low, a, b)


def local_kernel(pairs, x_ref, b_ref, tail_ref, meta_ref, out_ref):
    rows = x_ref.shape[0]
    tail = tail_ref[0]
    scaled = [
        (x_ref[:, PAIR * p : PAIR * (p + 1)].astype(F32) * pair_of(tail, p, rows)).astype(BF16)
        for p in range(pairs)
    ]
    state = lax.dot_general(
        b_ref[...],
        jnp.concatenate(scaled, axis=1),
        (((0,), (0,)), ((), ())),
        preferred_element_type=F32,
    )
    for p in range(pairs):
        out_ref[p, :STATE, :] = state[:, PAIR * p : PAIR * (p + 1)].astype(BF16)
        out_ref[p, STATE:, :] = meta_ref[p]


def local_states(x_in, in_b, tail, meta, groups, pairs):
    tok = x_in.shape[0]
    width = pairs * PAIR
    return pl.pallas_call(
        functools.partial(local_kernel, pairs),
        grid=(groups,),
        in_specs=[
            pl.BlockSpec((tok, width), lambda g: (0, g)),
            pl.BlockSpec((tok, STATE), lambda g: (0, g)),
            pl.BlockSpec((1, tok, 2 * pairs), lambda g: (g, 0, 0)),
            pl.BlockSpec((pairs, META, PAIR), lambda g: (g, 0, 0)),
        ],
        out_specs=pl.BlockSpec((pairs, STATE + META, PAIR), lambda g: (g, 0, 0)),
        out_shape=jax.ShapeDtypeStruct((groups * pairs, STATE + META, PAIR), BF16),
        name="local_states",
        compiler_params=pltpu.CompilerParams(vmem_limit_bytes=40 * 2**20),
    )(x_in, in_b, tail, meta)


def prefix_kernel(per, got_ref, out_ref):
    count = got_ref.shape[0] // per
    for q in range(per):
        state = jnp.zeros((STATE, PAIR), F32)
        for k in range(count):
            out_ref[k * per + q] = state.astype(BF16)
            block = got_ref[k * per + q].astype(F32)
            keep = jnp.exp(block[STATE : STATE + 1] + block[STATE + 1 : STATE + 2])
            state = state * keep + block[:STATE]


def prefix_states(got, per):
    return pl.pallas_call(
        functools.partial(prefix_kernel, per),
        out_shape=jax.ShapeDtypeStruct((got.shape[0], STATE, PAIR), BF16),
        name="prefix_states",
        compiler_params=pltpu.CompilerParams(vmem_limit_bytes=40 * 2**20),
    )(got)


def mixer_kernel(
    pairs,
    x_ref,
    gate_ref,
    b_ref,
    c_ref,
    cum_ref,
    cumt_ref,
    dt_ref,
    skip_ref,
    gain_ref,
    in_ref,
    y_ref,
    state,
    gated,
):
    rows = x_ref.shape[0]

    @pl.when(pl.program_id(1) == 0)
    def _():
        state[...] = in_ref[...].astype(F32)

    bmat, cmat = b_ref[...], c_ref[...]
    cb = lax.dot_general(cmat, bmat, (((1,), (1,)), ((), ())), preferred_element_type=F32)
    row = lax.broadcasted_iota(jnp.int32, (rows, rows), 0)
    col = lax.broadcasted_iota(jnp.int32, (rows, rows), 1)
    cb = jnp.where(row >= col, cb, 0.0)
    low = lax.broadcasted_iota(jnp.int32, (rows, PAIR), 1) < HEAD_DIM
    cum, dt, cumt = cum_ref[0], dt_ref[0], cumt_ref[...]
    square = jnp.zeros((rows, 1), F32)
    for p in range(pairs):
        lanes = slice(PAIR * p, PAIR * (p + 1))
        x = x_ref[:, lanes].astype(F32)
        left = jnp.broadcast_to(cum[:, 2 * p : 2 * p + 1], (rows, PAIR))
        right = jnp.broadcast_to(cum[:, 2 * p + 1 : 2 * p + 2], (rows, PAIR))
        w0 = cb * jnp.exp(jnp.minimum(left - cumt[2 * p : 2 * p + 1, :], 0.0))
        w1 = cb * jnp.exp(jnp.minimum(right - cumt[2 * p + 1 : 2 * p + 2, :], 0.0))
        both = jnp.where(low, left, right)
        last = both[rows - 1 : rows, :]
        stepped = x * pair_of(dt, p, rows)
        stacked = jnp.concatenate(
            [jnp.where(low, stepped, 0.0), jnp.where(low, 0.0, stepped)], axis=0
        ).astype(BF16)
        weights = jnp.concatenate([w0, w1], axis=1).astype(BF16)
        held = state[p]
        result = jnp.dot(weights, stacked, preferred_element_type=F32)
        result += jnp.exp(both) * jnp.dot(cmat, held.astype(BF16), preferred_element_type=F32)
        result += skip_ref[0:1, lanes] * x
        ending = (stepped * jnp.exp(last - both)).astype(BF16)
        state[p] = held * jnp.exp(last) + lax.dot_general(
            bmat, ending, (((0,), (0,)), ((), ())), preferred_element_type=F32
        )
        g = gate_ref[:, lanes].astype(F32)
        u = result * (g / (1.0 + jnp.exp(-g)))
        gated[:, lanes] = u
        square += jnp.sum(u * u, axis=1, keepdims=True)
    scale = lax.rsqrt(square * (1.0 / (pairs * PAIR)) + 1e-05)
    y_ref[...] = (gated[...] * scale * gain_ref[0:1, :]).astype(BF16)


def mixer(x_in, gate, in_b, in_c, cum, cumt, dt, skip, gain, incoming, groups, pairs):
    tok = x_in.shape[0]
    width = pairs * PAIR
    wide = pl.BlockSpec((CHUNK, width), lambda g, c: (c, g))
    maps = pl.BlockSpec((CHUNK, STATE), lambda g, c: (c, g))
    cols = pl.BlockSpec((1, CHUNK, 2 * pairs), lambda g, c: (g, c, 0))
    line = pl.BlockSpec((1, width), lambda g, c: (0, g))
    return pl.pallas_call(
        functools.partial(mixer_kernel, pairs),
        grid=(groups, tok // CHUNK),
        in_specs=[
            wide,
            wide,
            maps,
            maps,
            cols,
            pl.BlockSpec((2 * pairs, CHUNK), lambda g, c: (g, c)),
            cols,
            line,
            line,
            pl.BlockSpec((pairs, STATE, PAIR), lambda g, c: (g, 0, 0)),
        ],
        out_specs=wide,
        out_shape=jax.ShapeDtypeStruct((tok, groups * width), BF16),
        scratch_shapes=[pltpu.VMEM((pairs, STATE, PAIR), F32), pltpu.VMEM((CHUNK, width), F32)],
        name="mixer",
        compiler_params=pltpu.CompilerParams(vmem_limit_bytes=40 * 2**20),
    )(x_in, gate, in_b, in_c, cum, cumt, dt, skip, gain, incoming)


def on_device(
    x_in,
    gate_input,
    in_b,
    in_c,
    step_size,
    log_decay,
    skip_gain,
    norm_gain,
    out_weight,
    probe,
    span_start,
    span_len,
    span_owner,
    span_label,
):
    tok, inner = x_in.shape
    heads = step_size.shape[1]
    groups = in_b.shape[1] // STATE
    pairs = heads // groups // 2
    owners = lax.axis_size("seq")
    weight = lax.all_gather(out_weight, "seq", axis=1, tiled=True)

    high = lax.Precision.HIGHEST
    lower = jnp.tril(jnp.ones((CHUNK, CHUNK), F32))
    cum = jnp.einsum("ts,csh->cth", lower, log_decay.reshape(-1, CHUNK, heads), precision=high)
    ends = cum[:, -1, :]
    total = jnp.sum(ends, axis=0)
    chunks = tok // CHUNK
    behind = jnp.stack(
        [sum((ends[j] for j in range(c + 1, chunks)), jnp.zeros_like(total)) for c in range(chunks)]
    )
    tail = jnp.exp(ends[:, None] - cum + behind[:, None]).reshape(tok, heads) * step_size
    cum = cum.reshape(tok, heads)

    def by_group(a):
        return jnp.transpose(a.reshape(tok, groups, 2 * pairs), (1, 0, 2))

    total_high = lax.reduce_precision(total, 8, 7)
    total_low = total - total_high
    halves = jnp.stack([total_high, total_low])
    wide = jnp.repeat(halves.reshape(2, heads // 2, 2), HEAD_DIM, axis=2)
    meta = jnp.pad(jnp.transpose(wide, (1, 0, 2)), ((0, 0), (0, META - 2), (0, 0))).astype(BF16)
    local = local_states(x_in, in_b, by_group(tail), meta, groups, pairs)

    here = heads // 2
    share = -(-here // owners)
    if share * owners > here:
        local = jnp.pad(local, ((0, share * owners - here), (0, 0), (0, 0)))
    got = lax.all_to_all(local, "seq", split_axis=0, concat_axis=0, tiled=True)
    incoming = lax.all_to_all(
        prefix_states(got, share), "seq", split_axis=0, concat_axis=0, tiled=True
    )[:here]
    skip = jnp.repeat(skip_gain, HEAD_DIM)[None]
    y = mixer(
        x_in,
        gate_input,
        in_b,
        in_c,
        by_group(cum),
        cum.T,
        by_group(step_size),
        skip,
        norm_gain[None],
        incoming,
        groups,
        pairs,
    )

    base = lax.axis_index("seq") * tok
    prev_start, prev_len = from_behind((span_start, span_len), "seq", 1)
    place = base + jnp.arange(tok, dtype=jnp.int32)
    count = span_start.shape[0]
    masks = jnp.concatenate(
        [inside_mask(prev_start, prev_len, place), inside_mask(span_start, span_len, place)]
    )
    both = jnp.dot(masks, y, preferred_element_type=F32)
    returned = from_behind(both[:count].astype(BF16), "seq", -1)
    means = (both[count:] + returned.astype(F32)) / span_len[:, None].astype(F32)
    slots_total = owners * CAP
    owner = span_owner[:, 0]
    index = jnp.arange(count)
    earlier = index[None, :] < index[:, None]
    same = owner[:, None] == owner[None, :]
    slot = jnp.sum(jnp.logical_and(same, earlier), axis=1)
    pick = jnp.arange(slots_total, dtype=jnp.int32)[:, None] == (owner * CAP + slot)[None, :]
    sent = jnp.dot(pick.astype(BF16), means.astype(BF16), preferred_element_type=F32)
    labels = jnp.sum(jnp.where(pick, span_label[None, :] + 1, 0), axis=1) - 1
    got_means = lax.all_to_all(
        sent.astype(BF16).reshape(owners, CAP, -1), "seq", split_axis=0, concat_axis=0, tiled=True
    ).reshape(slots_total, -1)
    labels = lax.all_to_all(
        labels.reshape(owners, CAP), "seq", split_axis=0, concat_axis=0, tiled=True
    ).reshape(-1)
    valid = labels >= 0

    return project(jnp.concatenate([y, got_means], axis=0), weight, probe, tok, labels, valid)


def project_kernel(tok, rows_ref, weight_ref, out_ref, feature_ref):
    out = jnp.dot(rows_ref[...], weight_ref[...], preferred_element_type=F32)
    out_ref[...] = out[:tok].astype(BF16)
    feature_ref[...] = out[tok:].astype(BF16)


def project_rows(rows, weight, tok):
    count, inner = rows.shape
    model = weight.shape[1]
    width = 512
    return pl.pallas_call(
        functools.partial(project_kernel, tok),
        grid=(model // width,),
        in_specs=[
            pl.BlockSpec((count, inner), lambda n: (0, 0)),
            pl.BlockSpec((inner, width), lambda n: (0, n)),
        ],
        out_specs=[
            pl.BlockSpec((tok, width), lambda n: (0, n)),
            pl.BlockSpec((count - tok, width), lambda n: (0, n)),
        ],
        out_shape=[
            jax.ShapeDtypeStruct((tok, model), BF16),
            jax.ShapeDtypeStruct((count - tok, model), BF16),
        ],
        name="project_rows",
        compiler_params=pltpu.CompilerParams(vmem_limit_bytes=40 * 2**20),
    )(rows, weight)


def project(rows, weight, probe, tok, labels, valid):
    if lax.axis_size("head") > 1:
        out = jnp.dot(rows, weight, preferred_element_type=F32)
        layer_out = lax.psum_scatter(
            out[:tok].astype(BF16), "head", scatter_dimension=1, tiled=True
        )
        feature = lax.psum_scatter(out[tok:], "head", scatter_dimension=1, tiled=True)
        feature = feature.astype(BF16)
    else:
        layer_out, feature = project_rows(rows, weight, tok)
    logits = jnp.dot(feature, probe[0], preferred_element_type=F32)
    logits = lax.psum(logits, "head")
    top = jnp.max(logits, axis=1, keepdims=True)
    lse = top[:, 0] + jnp.log(jnp.sum(jnp.exp(logits - top), axis=1))
    onehot = jnp.arange(logits.shape[1])[None, :] == labels[:, None]
    picked = jnp.sum(jnp.where(onehot, logits, 0.0), axis=1)
    loss = jnp.where(valid, lse - picked, 0.0)
    probs = jnp.exp(logits - lse[:, None])
    resid = jnp.where(valid[:, None], probs - onehot.astype(F32), 0.0).astype(BF16)
    grad = jnp.dot(feature.T, resid, preferred_element_type=F32)
    return (layer_out, grad[None], loss[None])


def solution(mesh):
    placed = (
        P("seq", "head"),
        P("seq", "head"),
        P("seq", "head"),
        P("seq", "head"),
        P("seq", "head"),
        P("seq", "head"),
        P("head"),
        P("head"),
        P("head", "seq"),
        P("seq", "head", None),
        P("seq"),
        P("seq"),
        P("seq", None),
        P("seq"),
    )
    return jax.shard_map(
        on_device,
        mesh=mesh,
        in_specs=placed,
        out_specs=(P("seq", "head"), P("seq", "head", None), P("seq", None)),
        check_vma=False,
    )
```
